32 devices in a mesh: scen: 4 (over y, x), border: 8 (over z, core).
Axes of the slice: x: 2, y: 2, z: 4, core: 2. Of those that a mesh axis runs over, the one named last changes fastest.
Arguments:
- border: bfloat16 [8, 512, 32768], P('scen', None, 'border'), may hold values from -1.5 to 1.5
- blocks: float32 [8, 512, 512], P('scen'), may hold values from -60 to 64, as said below
- root_diag: float32 [32768], P('border'), may hold values from 4 to 128
- live_rows: int32 [8], P('scen'), may hold values from 128 to 512, as said below
- panel_ids: int32 [4], replicated, may hold values from 0 to 127
Outputs:
- root_rows: float32 [8, 4096, 1024], P('border', 'scen')
- factor: float32 [4, 256, 256], replicated
The draws below stay inside these ranges and needn't reach their ends.
Inputs may be any that keep to these rules, and one draw needn't show every extreme that they name: blocks[i] is a Gram matrix plus a positive diagonal of at least 1, hence symmetric positive definite. `live_rows`: each entry is a multiple of 128, and some scenario has 512.
All inputs are finite; a program needn't handle non-finite values.
Results may differ from the reference program's by a relative error of at most 0.0017.
Values may be sent and summed in bfloat16 or wider, within the bound.
A program may use at most 128 MiB of HBM per device.

```python
import math
import jax
import jax.numpy as jnp
from jax import lax

NS = 512
BCOL = 4096
PW = 256
PANELS = 4
SCEN = 8
NB = 32768
PR = 1024
NPANEL = 128
N_BORDER = 8


def draw_blocks(key, part):
    key_left = jax.random.fold_in(key, 11)
    key_diag = jax.random.fold_in(key, 12)
    key_spike = jax.random.fold_in(key, 13)
    key_scale = jax.random.fold_in(key, 14)
    factors = jax.random.truncated_normal(key_left, -3.0, 3.0, (SCEN, NS, NS), jnp.float32)
    gram = jnp.einsum('ikr,ijr->ikj', factors, factors, precision=lax.Precision.HIGHEST) / NS
    spike_cols = jax.random.uniform(key_spike, (SCEN, NS, 16), jnp.float32, -1.0, 1.0)
    spike_scale = jnp.exp(jax.random.uniform(key_scale, (SCEN, 16), jnp.float32, 0.0, 0.5 * jnp.log(10.0)))
    lifted = spike_cols * spike_scale[:, None, :]
    spikes = 0.3 * jnp.einsum('ikr,ijr->ikj', lifted, lifted, precision=lax.Precision.HIGHEST)
    diagonal = jnp.exp(jax.random.uniform(key_diag, (SCEN, NS), jnp.float32, 0.0, jnp.log(4.0)))
    eye_mat = jnp.eye(NS, dtype=jnp.float32)
    return gram + spikes + diagonal[:, :, None] * eye_mat[None, :, :]


def draw_live_rows(key, part):
    key_count = jax.random.fold_in(key, 21)
    key_full = jax.random.fold_in(key, 22)
    quarter = NS // 4
    counts = jax.random.randint(key_count, (SCEN,), 1, 5, jnp.int32) * quarter
    chosen = jax.random.randint(key_full, (), 0, SCEN, jnp.int32)
    return jnp.where(jnp.arange(SCEN, dtype=jnp.int32) == chosen, jnp.int32(NS), counts).astype(jnp.int32)


def plant(result, own_key, low, high):
    place = [jax.random.randint(jax.random.fold_in(own_key, axis), (), 0, length) for axis, length in enumerate(result.shape)]
    main_axis = result.shape.index(max(result.shape))
    neighbour = place[:main_axis] + [(place[main_axis] + 1) % result.shape[main_axis]] + place[main_axis + 1:]
    return result.at[tuple(place)].set(low).at[tuple(neighbour)].set(high)


def level_of(stream_key, extent, shards, least, largest):
    factor_of, own = 1.0, jax.random.fold_in(stream_key, 6)
    for dim, parts in shards:
        draws = jnp.exp(jax.random.uniform(jax.random.fold_in(own, dim), (parts,), jnp.float32, least / len(shards), largest / len(shards)))
        factor_of = factor_of * jnp.repeat(draws, extent[dim] // parts).reshape([-1 if axis == dim else 1 for axis in range(len(extent))])
    return factor_of


def noise(own_key, shape, scale, bound, pieces=(), kind=jnp.bfloat16):
    factor_of = level_of(own_key, shape, pieces, -0.22, 0.18) if pieces else 1.0
    result = jax.random.normal(own_key, shape, jnp.float32) * scale * factor_of
    return jnp.minimum(jnp.maximum(result, -bound), bound).astype(kind)


def setup_inputs(seed: int = 0) -> dict:
    seeds = jax.random.split(jax.random.key(seed), 6)
    return {
        "border": noise(seeds[0], (SCEN, NS, NB), 0.25, 1.5, ((0, 4), (2, 8))),
        "blocks": draw_blocks(jax.random.fold_in(seeds[5], 71), 0),
        "root_diag": jnp.clip(jnp.exp(math.log(128.0) - 3.465736 * jax.random.uniform(seeds[2], (NB,), jnp.float32) ** level_of(seeds[2], (NB,), ((0, 8),), -0.2, 0.2)), 4.0, 128.0),
        "live_rows": draw_live_rows(jax.random.fold_in(seeds[5], 71), 0),
        "panel_ids": plant(jax.random.randint(seeds[4], (PANELS,), 0, NPANEL), jax.random.fold_in(seeds[4], 1), 0, NPANEL - 1).astype(jnp.int32),
    }


def reference(border, blocks, root_diag, live_rows, panel_ids):
    panel_cols = (panel_ids[:, None] * PW + jnp.arange(PW, dtype=jnp.int32)[None, :]).reshape(-1).astype(jnp.int32)
    levels = jnp.arange(NS, dtype=jnp.int32)
    identity = jnp.eye(NS, dtype=jnp.float32)

    def one_scenario(total, item):
        rows_in, block, live = item
        keep = levels >= NS - live
        masked = jnp.where(keep[:, None], rows_in, jnp.zeros_like(rows_in))
        lower_factor = jnp.linalg.cholesky(block)
        inverse = lax.linalg.triangular_solve(lower_factor, identity, left_side=True, lower=True).astype(jnp.bfloat16)
        solved = jnp.dot(inverse.astype(jnp.float32), masked.astype(jnp.float32), preferred_element_type=jnp.float32).astype(jnp.bfloat16)
        panels = jnp.take(solved, panel_cols, axis=1)
        total = total + jnp.dot(panels.T.astype(jnp.float32), solved.astype(jnp.float32), preferred_element_type=jnp.float32)
        return (total, None)
    schur, unused = lax.scan(one_scenario, jnp.zeros((PR, NB), jnp.float32), (border, blocks, live_rows))
    columns = jnp.arange(NB, dtype=jnp.int32)
    schur = schur + jnp.where(columns[None, :] == panel_cols[:, None], root_diag[None, :], jnp.zeros((), jnp.float32))
    tiles = []
    for position in range(PANELS):
        row_start = jnp.asarray(position * PW, jnp.int32)
        col_start = (panel_ids[position] * PW).astype(jnp.int32)
        tiles.append(lax.dynamic_slice(schur, (row_start, col_start), (PW, PW)))
    diag_block = jnp.stack(tiles)
    factor = jnp.linalg.cholesky(diag_block)
    eye_stack = jnp.broadcast_to(jnp.eye(PW, dtype=jnp.float32), diag_block.shape)
    factor_inverse = lax.linalg.triangular_solve(factor, eye_stack, left_side=True, lower=True)
    solved_rows = jnp.einsum('pkj,pjc->pkc', factor_inverse, schur.reshape(PANELS, PW, NB), precision=lax.Precision.HIGHEST)
    root_rows = solved_rows.reshape(PR, N_BORDER, BCOL).transpose(1, 2, 0)
    return (root_rows, factor)
```

```python
import functools

import jax
import jax.numpy as jnp
from jax import lax
from jax.experimental import pallas as pl
from jax.experimental.pallas import tpu as pltpu
from jax.sharding import PartitionSpec as P

PW = 256
PANELS = 4
BLK = 128
SUB = 8


def eliminate(mats):
    lane1 = lax.broadcasted_iota(jnp.int32, (1, BLK), 1)
    sub8 = lax.broadcasted_iota(jnp.int32, (SUB, BLK), 0)
    lane8 = lax.broadcasted_iota(jnp.int32, (SUB, BLK), 1)
    rests = list(mats)
    done = [[] for _ in mats]
    for group in range(BLK // SUB):
        base = group * SUB
        rows = BLK - base
        cols = [
            [jnp.broadcast_to(rest[:, base + t : base + t + 1], (rows, BLK)) for t in range(SUB)]
            for rest in rests
        ]
        tops = [rest[:SUB] for rest in rests]
        lows = [rest[SUB:] for rest in rests]
        if rows > SUB:
            wide = lax.broadcasted_iota(jnp.int32, (rows - SUB, BLK), 1)
            inside = (wide >= base) & (wide < base + SUB)
            lows = [jnp.where(inside, 0.0, low) for low in lows]
        pivots = [jnp.ones((SUB, BLK), jnp.float32) for _ in mats]
        for t in range(SUB):
            for m in range(len(mats)):
                col = cols[m][t]
                pivot = col[t : t + 1, :]
                scaled = col * (1.0 / pivot)
                top = tops[m]
                row = jnp.where(lane1 == base + t, 1.0, top[t : t + 1, :])
                below = sub8 > t
                cleared = jnp.where(
                    lane8 == base + t, jnp.where(below, 0.0, 1.0), top
                )
                cleared = jnp.where((lane8 == base + t) & (sub8 < t), top, cleared)
                tops[m] = cleared - jnp.where(below, scaled[:SUB], 0.0) * row
                pivots[m] = jnp.where(sub8 == t, pivot, pivots[m])
                if rows > SUB:
                    later = (lane1 > base + t) & (lane1 < base + SUB)
                    lows[m] = lows[m] - scaled[SUB:] * jnp.where(later, 0.0, row)
                for s in range(t + 1, SUB):
                    cols[m][s] = cols[m][s] - scaled * col[s : s + 1, :]
        for m in range(len(mats)):
            done[m].append(tops[m] * lax.rsqrt(pivots[m]))
        rests = lows
    return [jnp.concatenate(part, axis=0) for part in done]


def mxu(left, right, dims):
    return lax.dot_general(
        left, right, (dims, ((), ())),
        precision=lax.Precision.HIGHEST, preferred_element_type=jnp.float32,
    )


def factor_kernel(count, order, want_lower, in_ref, *refs):
    if want_lower:
        inv_ref, low_ref, work = refs
    else:
        inv_ref, work = refs
    steps = order // BLK
    work[...] = in_ref[...]
    eye = (
        lax.broadcasted_iota(jnp.int32, (BLK, BLK), 0)
        == lax.broadcasted_iota(jnp.int32, (BLK, BLK), 1)
    ).astype(jnp.float32)
    tril = lax.broadcasted_iota(jnp.int32, (BLK, BLK), 0) >= lax.broadcasted_iota(
        jnp.int32, (BLK, BLK), 1
    )

    @pl.loop(0, steps)
    def _(step):
        here = pl.ds(pl.multiple_of(step * BLK, BLK), BLK)
        blocks = eliminate([work[m, here, here] for m in range(count)])
        for m in range(count):
            inverse = jnp.where(tril, blocks[m], 0.0)
            work[m, here, here] = eye
            panel = mxu(inverse, work[m, here, :], ((1,), (0,)))
            work[m, here, :] = panel
            for i in range(1, steps):
                mine = slice(i * BLK, (i + 1) * BLK)

                @pl.when(i > step)
                def _():
                    work[m, mine, here] = jnp.zeros((BLK, BLK), jnp.float32)
                    work[m, mine, :] = work[m, mine, :] - mxu(
                        panel[:, mine], panel, ((0,), (0,))
                    )

            work[m, here, here] = blocks[m]

    row = lax.broadcasted_iota(jnp.int32, (order, order), 0)
    col = lax.broadcasted_iota(jnp.int32, (order, order), 1)
    for m in range(count):
        full = work[m]
        inv_ref[m] = jnp.where(row >= col, full, 0.0).astype(inv_ref.dtype)
        if want_lower:
            low_ref[m] = jnp.where(
                row > col, full.T, jnp.where(row == col, 1.0 / full, 0.0)
            )


def factor_blocks(blocks, inv_type, want_lower):
    count, order, _ = blocks.shape
    out = [jax.ShapeDtypeStruct(blocks.shape, inv_type)]
    if want_lower:
        out.append(jax.ShapeDtypeStruct(blocks.shape, jnp.float32))
    return pl.pallas_call(
        functools.partial(factor_kernel, count, order, want_lower),
        out_shape=tuple(out),
        in_specs=[pl.BlockSpec(memory_space=pltpu.VMEM)],
        out_specs=tuple(pl.BlockSpec(memory_space=pltpu.VMEM) for _ in out),
        scratch_shapes=[pltpu.VMEM(blocks.shape, jnp.float32)],
        compiler_params=pltpu.CompilerParams(vmem_limit_bytes=40 * 1024 * 1024),
        cost_estimate=pl.CostEstimate(
            flops=count * order**3 * 60, bytes_accessed=count * order * order * 16,
            transcendentals=0,
        ),
    )(blocks)


def on_device(border, blocks, root_diag, live_rows, panel_ids):
    scen_local, order, width = border.shape
    scen_count = lax.axis_size("scen")
    share = width // scen_count
    border_pos = lax.axis_index("border")
    scen_pos = lax.axis_index("scen")
    slabs = width // PW
    levels = jnp.arange(order, dtype=jnp.int32)

    raw = []
    diag = []
    for position in range(PANELS):
        chosen = panel_ids[position]
        mine = chosen // slabs == border_pos
        offset = chosen % slabs * PW
        cols = lax.dynamic_slice_in_dim(border, offset, PW, 2)
        raw.append(jnp.where(mine, cols, jnp.zeros_like(cols)))
        piece = lax.dynamic_slice_in_dim(root_diag, offset, PW)
        diag.append(jnp.where(mine, piece, jnp.zeros_like(piece)))
    window = lax.psum(jnp.concatenate(raw, axis=2), "border")
    window_diag = lax.psum(jnp.stack(diag), "border")
    window = lax.all_gather(window, "scen", axis=0, tiled=True)

    def piece_of(index):
        return lax.dynamic_slice_in_dim(border, index * share, share, 2)

    pieces = [piece_of(scen_pos)]
    for step in range(1, scen_count):
        pieces.append(
            lax.ppermute(
                piece_of((scen_pos + step) % scen_count),
                "scen",
                [(i, (i + step) % scen_count) for i in range(scen_count)],
            )
        )

    (inverse,) = factor_blocks(blocks, jnp.bfloat16, False)
    inverses = lax.all_gather(inverse, "scen", axis=0, tiled=True)
    lives = lax.all_gather(live_rows, "scen", axis=0, tiled=True)

    def solve(inv, live, columns):
        keep = levels[None, :, None] >= (order - live)[:, None, None]
        masked = jnp.where(keep, columns, jnp.zeros_like(columns))
        return jnp.einsum(
            "ikr,irc->ikc", inv, masked, preferred_element_type=jnp.float32
        ).astype(jnp.bfloat16)

    panels = solve(inverses, lives, window)
    diag_block = jnp.stack(
        [
            lax.dot_general(
                panels[:, :, p * PW : (p + 1) * PW],
                panels[:, :, p * PW : (p + 1) * PW],
                (((0, 1), (0, 1)), ((), ())),
                preferred_element_type=jnp.float32,
            )
            for p in range(PANELS)
        ]
    )
    eye = jnp.eye(PW, dtype=jnp.float32)
    diag_block = diag_block + window_diag[:, :, None] * eye[None]
    factor_inverse, factor = factor_blocks(diag_block, jnp.float32, True)

    schur_cols = jnp.zeros((share, PANELS * PW), jnp.float32)
    for step in range(scen_count):
        source = (scen_pos - step) % scen_count
        inv = lax.dynamic_slice_in_dim(inverses, source * scen_local, scen_local, 0)
        live = lax.dynamic_slice_in_dim(lives, source * scen_local, scen_local, 0)
        own = lax.dynamic_slice_in_dim(panels, source * scen_local, scen_local, 0)
        solved = solve(inv, live, pieces[step])
        schur_cols = schur_cols + lax.dot_general(
            solved, own, (((0, 1), (0, 1)), ((), ())), preferred_element_type=jnp.float32
        )
    base = border_pos * width + scen_pos * share
    global_cols = base + jnp.arange(share, dtype=jnp.int32)
    window_cols = (panel_ids[:, None] * PW + jnp.arange(PW, dtype=jnp.int32)[None, :]).reshape(-1)
    diag_part = lax.dynamic_slice_in_dim(root_diag, scen_pos * share, share)
    matches = global_cols[:, None] == window_cols[None, :]
    schur_cols = schur_cols + jnp.where(matches, diag_part[:, None], jnp.zeros((), jnp.float32))
    shaped = schur_cols.reshape(share, PANELS, PW)
    solved_rows = jnp.einsum(
        "cpj,pkj->cpk", shaped, factor_inverse, precision=lax.Precision.HIGH
    )
    return (solved_rows.reshape(1, share, PANELS * PW), factor)


def solution(mesh):
    placed = (P("scen", None, "border"), P("scen", None, None), P("border"), P("scen"), P())
    return jax.shard_map(
        on_device,
        mesh=mesh,
        in_specs=placed,
        out_specs=(P("border", "scen", None), P()),
        check_vma=False,
    )
```

```python
import functools

import jax
import jax.numpy as jnp
from jax import lax
from jax.experimental import pallas as pl
from jax.experimental.pallas import tpu as pltpu
from jax.sharding import PartitionSpec as P

PW = 256
PANELS = 4
BLK = 128
SUB = 8


def eliminate(mats):
    lane1 = lax.broadcasted_iota(jnp.int32, (1, BLK), 1)
    sub8 = lax.broadcasted_iota(jnp.int32, (SUB, BLK), 0)
    lane8 = lax.broadcasted_iota(jnp.int32, (SUB, BLK), 1)
    rests = list(mats)
    done = [[] for _ in mats]
    for group in range(BLK // SUB):
        base = group * SUB
        rows = BLK - base
        cols = [
            [jnp.broadcast_to(rest[:, base + t : base + t + 1], (rows, BLK)) for t in range(SUB)]
            for rest in rests
        ]
        tops = [rest[:SUB] for rest in rests]
        lows = [rest[SUB:] for rest in rests]
        if rows > SUB:
            wide = lax.broadcasted_iota(jnp.int32, (rows - SUB, BLK), 1)
            inside = (wide >= base) & (wide < base + SUB)
            lows = [jnp.where(inside, 0.0, low) for low in lows]
        pivots = [jnp.ones((SUB, BLK), jnp.float32) for _ in mats]
        for t in range(SUB):
            for m in range(len(mats)):
                col = cols[m][t]
                pivot = col[t : t + 1, :]
                scaled = col * (1.0 / pivot)
                top = tops[m]
                row = jnp.where(lane1 == base + t, 1.0, top[t : t + 1, :])
                below = sub8 > t
                cleared = jnp.where(
                    lane8 == base + t, jnp.where(below, 0.0, 1.0), top
                )
                cleared = jnp.where((lane8 == base + t) & (sub8 < t), top, cleared)
                tops[m] = cleared - jnp.where(below, scaled[:SUB], 0.0) * row
                pivots[m] = jnp.where(sub8 == t, pivot, pivots[m])
                if rows > SUB:
                    later = (lane1 > base + t) & (lane1 < base + SUB)
                    lows[m] = lows[m] - scaled[SUB:] * jnp.where(later, 0.0, row)
                for s in range(t + 1, SUB):
                    cols[m][s] = cols[m][s] - scaled * col[s : s + 1, :]
        for m in range(len(mats)):
            done[m].append(tops[m] * lax.rsqrt(pivots[m]))
        rests = lows
    return [jnp.concatenate(part, axis=0) for part in done]


def mxu(left, right, dims):
    return lax.dot_general(
        left, right, (dims, ((), ())),
        precision=lax.Precision.HIGHEST, preferred_element_type=jnp.float32,
    )


def factor_kernel(count, order, want_lower, in_ref, *refs):
    if want_lower:
        inv_ref, low_ref, work = refs
    else:
        inv_ref, work = refs
    steps = order // BLK
    work[...] = in_ref[...]
    eye = (
        lax.broadcasted_iota(jnp.int32, (BLK, BLK), 0)
        == lax.broadcasted_iota(jnp.int32, (BLK, BLK), 1)
    ).astype(jnp.float32)
    tril = lax.broadcasted_iota(jnp.int32, (BLK, BLK), 0) >= lax.broadcasted_iota(
        jnp.int32, (BLK, BLK), 1
    )

    @pl.loop(0, steps)
    def _(step):
        here = pl.ds(pl.multiple_of(step * BLK, BLK), BLK)
        blocks = eliminate([work[m, here, here] for m in range(count)])
        for m in range(count):
            inverse = jnp.where(tril, blocks[m], 0.0)
            work[m, here, here] = eye
            panel = mxu(inverse, work[m, here, :], ((1,), (0,)))
            work[m, here, :] = panel
            for i in range(1, steps):
                mine = slice(i * BLK, (i + 1) * BLK)

                @pl.when(i > step)
                def _():
                    work[m, mine, here] = jnp.zeros((BLK, BLK), jnp.float32)
                    work[m, mine, :] = work[m, mine, :] - mxu(
                        panel[:, mine], panel, ((0,), (0,))
                    )

            work[m, here, here] = blocks[m]

    row = lax.broadcasted_iota(jnp.int32, (order, order), 0)
    col = lax.broadcasted_iota(jnp.int32, (order, order), 1)
    for m in range(count):
        full = work[m]
        inv_ref[m] = jnp.where(row >= col, full, 0.0).astype(inv_ref.dtype)
        if want_lower:
            low_ref[m] = jnp.where(
                row > col, full.T, jnp.where(row == col, 1.0 / full, 0.0)
            )


def factor_blocks(blocks, inv_type, want_lower):
    count, order, _ = blocks.shape
    out = [jax.ShapeDtypeStruct(blocks.shape, inv_type)]
    if want_lower:
        out.append(jax.ShapeDtypeStruct(blocks.shape, jnp.float32))
    return pl.pallas_call(
        functools.partial(factor_kernel, count, order, want_lower),
        out_shape=tuple(out),
        in_specs=[pl.BlockSpec(memory_space=pltpu.VMEM)],
        out_specs=tuple(pl.BlockSpec(memory_space=pltpu.VMEM) for _ in out),
        scratch_shapes=[pltpu.VMEM(blocks.shape, jnp.float32)],
        compiler_params=pltpu.CompilerParams(vmem_limit_bytes=40 * 1024 * 1024),
        cost_estimate=pl.CostEstimate(
            flops=count * order**3 * 60, bytes_accessed=count * order * order * 16,
            transcendentals=0,
        ),
    )(blocks)


def cut(array, start, size, axis):
    return lax.dynamic_slice_in_dim(array, start, size, axis, allow_negative_indices=False)


def split3(value):
    high = value.astype(jnp.bfloat16)
    rest = value - high.astype(jnp.float32)
    middle = rest.astype(jnp.bfloat16)
    low = (rest - middle.astype(jnp.float32)).astype(jnp.bfloat16)
    return jnp.stack([high, middle, low])


def pack(inverse):
    half = inverse.shape[1] // 2
    return jnp.concatenate([inverse[:, :half, :half], inverse[:, half:, :]], axis=2)


def unpack(packed):
    half = packed.shape[1]
    top = jnp.concatenate([packed[:, :, :half], jnp.zeros_like(packed[:, :, :half])], axis=2)
    return jnp.concatenate([top, packed[:, :, half:]], axis=1)


def on_device(border, blocks, root_diag, live_rows, panel_ids):
    scen_local, order, width = border.shape
    scen_count = lax.axis_size("scen")
    far = scen_count - 1
    share = width // scen_count
    border_pos = lax.axis_index("border")
    scen_pos = lax.axis_index("scen")
    slabs = width // PW
    levels = jnp.arange(order, dtype=jnp.int32)
    keep = levels[None, :, None] >= (order - live_rows)[:, None, None]

    def swap(value, step):
        return lax.ppermute(value, "scen", [(i, i ^ step) for i in range(scen_count)])

    def piece_of(step):
        cols = cut(border, (scen_pos ^ step) * share, share, 2)
        return jnp.where(keep, cols, jnp.zeros_like(cols))

    def solve(inv, columns):
        return jnp.einsum(
            "ikr,irc->ikc", inv, columns, preferred_element_type=jnp.float32
        ).astype(jnp.bfloat16)

    raws = [swap(piece_of(step), step) for step in range(1, far)]

    window = []
    diag = []
    for position in range(PANELS):
        chosen = panel_ids[position]
        mine = lax.div(chosen, slabs) == border_pos
        offset = lax.rem(chosen, slabs) * PW
        cols = cut(border, offset, PW, 2)
        window.append(jnp.where(keep & mine, cols, jnp.zeros_like(cols)))
        part = cut(root_diag, offset, PW, 0)
        diag.append(jnp.where(mine, part, jnp.zeros_like(part)))
    parts = split3(jnp.concatenate(diag))
    extra = jnp.zeros((scen_local, 16, PANELS * PW), jnp.bfloat16).at[0, :3].set(parts)
    window = jnp.concatenate([jnp.concatenate(window, axis=2), extra], axis=1)
    window = lax.psum(window, "border")
    window_diag = jnp.sum(window[0, order : order + 3].astype(jnp.float32), axis=0)
    window = window[:, :order]

    (inverse,) = factor_blocks(blocks, jnp.bfloat16, False)
    inverse, raws = lax.optimization_barrier((inverse, raws))
    packed = pack(inverse)
    inverses = [unpack(swap(packed, step)) for step in range(1, far)]
    solved_far = swap(solve(inverse, piece_of(far)), far)
    solved = [solve(inverse, piece_of(0))]
    solved += [solve(inv, raw) for inv, raw in zip(inverses, raws)]
    solved.append(solved_far)

    own = solve(inverse, window)
    panels = [own] + [swap(own, step) for step in range(1, scen_count)]
    both = (((0, 1), (0, 1)), ((), ()))

    def diag_of(p):
        total = jnp.zeros((PW, PW), jnp.float32)
        for panel in panels:
            cols = panel[:, :, p * PW : (p + 1) * PW]
            total = total + lax.dot_general(cols, cols, both, preferred_element_type=jnp.float32)
        return total

    eye = jnp.eye(PW, dtype=jnp.float32)
    diag_block = jnp.stack([diag_of(p) for p in range(PANELS)])
    diag_block = diag_block + window_diag.reshape(PANELS, PW)[:, :, None] * eye[None]
    factor_inverse, factor = factor_blocks(diag_block, jnp.float32, True)

    base = border_pos * width + scen_pos * share
    global_cols = base + jnp.arange(share, dtype=jnp.int32)
    window_cols = (panel_ids[:, None] * PW + jnp.arange(PW, dtype=jnp.int32)[None, :]).reshape(-1)
    diag_part = cut(root_diag, scen_pos * share, share, 0)
    matches = global_cols[:, None] == window_cols[None, :]
    schur_cols = jnp.where(matches, diag_part[:, None], jnp.zeros((), jnp.float32))
    for left, right in zip(solved, panels):
        schur_cols = schur_cols + lax.dot_general(
            left, right, both, preferred_element_type=jnp.float32
        )
    shaped = schur_cols.reshape(share, PANELS, PW)
    solved_rows = jnp.einsum(
        "cpj,pkj->cpk", shaped, factor_inverse, precision=lax.Precision.HIGH
    )
    return (solved_rows.reshape(1, share, PANELS * PW), factor)


def solution(mesh):
    placed = (P("scen", None, "border"), P("scen", None, None), P("border"), P("scen"), P())
    return jax.shard_map(
        on_device,
        mesh=mesh,
        in_specs=placed,
        out_specs=(P("border", "scen", None), P()),
        check_vma=False,
    )
```

```python
import functools

import jax
import jax.numpy as jnp
from jax import lax
from jax.experimental import pallas as pl
from jax.experimental.pallas import tpu as pltpu
from jax.sharding import PartitionSpec as P

PW = 256
PANELS = 4
BLK = 128
SUB = 8


def eliminate(mats):
    lane1 = lax.broadcasted_iota(jnp.int32, (1, BLK), 1)
    sub8 = lax.broadcasted_iota(jnp.int32, (SUB, BLK), 0)
    lane8 = lax.broadcasted_iota(jnp.int32, (SUB, BLK), 1)
    rests = list(mats)
    done = [[] for _ in mats]
    for group in range(BLK // SUB):
        base = group * SUB
        rows = BLK - base
        cols = [
            [jnp.broadcast_to(rest[:, base + t : base + t + 1], (rows, BLK)) for t in range(SUB)]
            for rest in rests
        ]
        tops = [rest[:SUB] for rest in rests]
        lows = [rest[SUB:] for rest in rests]
        if rows > SUB:
            wide = lax.broadcasted_iota(jnp.int32, (rows - SUB, BLK), 1)
            inside = (wide >= base) & (wide < base + SUB)
            lows = [jnp.where(inside, 0.0, low) for low in lows]
        pivots = [jnp.ones((SUB, BLK), jnp.float32) for _ in mats]
        for t in range(SUB):
            for m in range(len(mats)):
                col = cols[m][t]
                pivot = col[t : t + 1, :]
                scaled = col * (1.0 / pivot)
                top = tops[m]
                row = jnp.where(lane1 == base + t, 1.0, top[t : t + 1, :])
                below = sub8 > t
                cleared = jnp.where(
                    lane8 == base + t, jnp.where(below, 0.0, 1.0), top
                )
                cleared = jnp.where((lane8 == base + t) & (sub8 < t), top, cleared)
                tops[m] = cleared - jnp.where(below, scaled[:SUB], 0.0) * row
                pivots[m] = jnp.where(sub8 == t, pivot, pivots[m])
                if rows > SUB:
                    later = (lane1 > base + t) & (lane1 < base + SUB)
                    lows[m] = lows[m] - scaled[SUB:] * jnp.where(later, 0.0, row)
                for s in range(t + 1, SUB):
                    cols[m][s] = cols[m][s] - scaled * col[s : s + 1, :]
        for m in range(len(mats)):
            done[m].append(tops[m] * lax.rsqrt(pivots[m]))
        rests = lows
    return [jnp.concatenate(part, axis=0) for part in done]


def mxu(left, right, dims):
    return lax.dot_general(
        left, right, (dims, ((), ())),
        precision=lax.Precision.HIGHEST, preferred_element_type=jnp.float32,
    )


def first_kernel(count, order, in_ref, inv_ref, work):
    work[...] = in_ref[...]
    factor_in_place(count, order, work, inv_ref, None)


def second_kernel(count, order, diag_ref, *refs):
    *panel_refs, inv_ref, low_ref, work = refs
    row = lax.broadcasted_iota(jnp.int32, (order, order), 0)
    col = lax.broadcasted_iota(jnp.int32, (order, order), 1)
    for p in range(count):
        total = jnp.where(row == col, diag_ref[p : p + 1, :], 0.0)
        for ref in panel_refs:
            for i in range(ref.shape[0]):
                cols = ref[i, :, p * order : (p + 1) * order]
                total = total + lax.dot_general(
                    cols, cols, (((0,), (0,)), ((), ())), preferred_element_type=jnp.float32
                )
        work[p] = total
    factor_in_place(count, order, work, inv_ref, low_ref)


def factor_in_place(count, order, work, inv_ref, low_ref):
    steps = order // BLK
    eye = (
        lax.broadcasted_iota(jnp.int32, (BLK, BLK), 0)
        == lax.broadcasted_iota(jnp.int32, (BLK, BLK), 1)
    ).astype(jnp.float32)
    tril = lax.broadcasted_iota(jnp.int32, (BLK, BLK), 0) >= lax.broadcasted_iota(
        jnp.int32, (BLK, BLK), 1
    )

    @pl.loop(0, steps)
    def _(step):
        here = pl.ds(pl.multiple_of(step * BLK, BLK), BLK)
        blocks = eliminate([work[m, here, here] for m in range(count)])
        for m in range(count):
            inverse = jnp.where(tril, blocks[m], 0.0)
            work[m, here, here] = eye
            panel = mxu(inverse, work[m, here, :], ((1,), (0,)))
            work[m, here, :] = panel
            for i in range(1, steps):
                mine = slice(i * BLK, (i + 1) * BLK)

                @pl.when(i > step)
                def _():
                    work[m, mine, here] = jnp.zeros((BLK, BLK), jnp.float32)
                    work[m, mine, :] = work[m, mine, :] - mxu(
                        panel[:, mine], panel, ((0,), (0,))
                    )

            work[m, here, here] = blocks[m]

    row = lax.broadcasted_iota(jnp.int32, (order, order), 0)
    col = lax.broadcasted_iota(jnp.int32, (order, order), 1)
    for m in range(count):
        full = work[m]
        inv_ref[m] = jnp.where(row >= col, full, 0.0).astype(inv_ref.dtype)
        if low_ref is not None:
            low_ref[m] = jnp.where(
                row > col, full.T, jnp.where(row == col, 1.0 / full, 0.0)
            )


def factor_call(body, count, order, args, inv_type, want_lower):
    shape = (count, order, order)
    out = [jax.ShapeDtypeStruct(shape, inv_type)]
    if want_lower:
        out.append(jax.ShapeDtypeStruct(shape, jnp.float32))
    return pl.pallas_call(
        functools.partial(body, count, order),
        out_shape=tuple(out),
        in_specs=[pl.BlockSpec(memory_space=pltpu.VMEM) for _ in args],
        out_specs=tuple(pl.BlockSpec(memory_space=pltpu.VMEM) for _ in out),
        scratch_shapes=[pltpu.VMEM(shape, jnp.float32)],
        compiler_params=pltpu.CompilerParams(vmem_limit_bytes=40 * 1024 * 1024),
        cost_estimate=pl.CostEstimate(
            flops=30 * 10**9, bytes_accessed=count * order * order * 16, transcendentals=0
        ),
    )(*args)


def rows_kernel(pairs, half, core_ref, diag_ref, window_ref, inv_ref, *refs):
    *refs, out_ref = refs
    solved, panels = refs[:pairs], refs[pairs:]
    cols = out_ref.shape[1]
    core = core_ref[0]
    place = lax.broadcasted_iota(jnp.int32, (cols, 1), 0) + pl.program_id(0) * cols
    total = jnp.where(place == window_ref[...], diag_ref[...], 0.0)

    def gram(left, right):
        return lax.dot_general(
            left, right, (((0,), (0,)), ((), ())), preferred_element_type=jnp.float32
        )

    for i in range(2 * half):
        total = total + gram(solved[0][i], panels[0][i])
    for k in range(1, pairs):
        mine, other = panels[2 * k - 1], panels[2 * k]
        for i in range(half):
            total = total + gram(solved[k][core * half + i], mine[i])
            total = total + gram(solved[k][(1 - core) * half + i], other[i])

    def parts(value):
        high = value.astype(jnp.bfloat16)
        return high, (value - high.astype(jnp.float32)).astype(jnp.bfloat16)

    def times(left, right):
        return lax.dot_general(
            left, right, (((1,), (1,)), ((), ())), preferred_element_type=jnp.float32
        )

    order = inv_ref.shape[1]
    for p in range(inv_ref.shape[0]):
        here = slice(p * order, (p + 1) * order)
        left_high, left_low = parts(total[:, here])
        high, low = parts(inv_ref[p])
        out_ref[0, :, here] = (
            times(left_low, high) + times(left_high, low) + times(left_high, high)
        )


def root_rows(core, diag, window, inverse, solved, panels):
    local, order, share = solved[0].shape
    cols = min(share, 256)
    whole = pl.BlockSpec(memory_space=pltpu.VMEM)
    return pl.pallas_call(
        functools.partial(rows_kernel, len(solved), local // 2),
        grid=(share // cols,),
        out_shape=jax.ShapeDtypeStruct((1, share, window.shape[1]), jnp.float32),
        in_specs=[
            pl.BlockSpec(memory_space=pltpu.SMEM),
            pl.BlockSpec((cols, 1), lambda i: (i, 0)),
            whole,
            whole,
        ]
        + [pl.BlockSpec((local, order, cols), lambda i: (0, 0, i)) for _ in solved]
        + [whole for _ in panels],
        out_specs=pl.BlockSpec((1, cols, window.shape[1]), lambda i: (0, i, 0)),
        compiler_params=pltpu.CompilerParams(vmem_limit_bytes=48 * 1024 * 1024),
        cost_estimate=pl.CostEstimate(
            flops=12 * 10**9, bytes_accessed=20 * 1024 * 1024, transcendentals=0
        ),
    )(core, diag, window, inverse, *solved, *panels)


def cut(array, start, size, axis):
    return lax.dynamic_slice_in_dim(array, start, size, axis, allow_negative_indices=False)


def split3(value):
    high = value.astype(jnp.bfloat16)
    rest = value - high.astype(jnp.float32)
    middle = rest.astype(jnp.bfloat16)
    low = (rest - middle.astype(jnp.float32)).astype(jnp.bfloat16)
    return jnp.stack([high, middle, low])


def pack(inverse):
    half = inverse.shape[1] // 2
    return jnp.concatenate([inverse[:, :half, :half], inverse[:, half:, :]], axis=2)


def unpack(packed):
    half = packed.shape[1]
    top = jnp.concatenate([packed[:, :, :half], jnp.zeros_like(packed[:, :, :half])], axis=2)
    return jnp.concatenate([top, packed[:, :, half:]], axis=1)


def on_device(border, blocks, root_diag, live_rows, panel_ids):
    scen_local, order, width = border.shape
    scen_count = lax.axis_size("scen")
    far = scen_count - 1
    share = width // scen_count
    border_pos = lax.axis_index("border")
    scen_pos = lax.axis_index("scen")
    slabs = width // PW
    levels = jnp.arange(order, dtype=jnp.int32)
    keep = levels[None, :, None] >= (order - live_rows)[:, None, None]

    def swap(value, step):
        return lax.ppermute(value, "scen", [(i, i ^ step) for i in range(scen_count)])

    def piece_of(step):
        cols = cut(border, (scen_pos ^ step) * share, share, 2)
        return jnp.where(keep, cols, jnp.zeros_like(cols))

    def solve(inv, columns):
        return jnp.einsum(
            "ikr,irc->ikc", inv, columns, preferred_element_type=jnp.float32
        ).astype(jnp.bfloat16)

    raws = [swap(piece_of(step), step) for step in range(1, far)]

    window = []
    diag = []
    for position in range(PANELS):
        chosen = panel_ids[position]
        mine = lax.div(chosen, slabs) == border_pos
        offset = lax.rem(chosen, slabs) * PW
        cols = cut(border, offset, PW, 2)
        window.append(jnp.where(keep & mine, cols, jnp.zeros_like(cols)))
        part = cut(root_diag, offset, PW, 0)
        diag.append(jnp.where(mine, part, jnp.zeros_like(part)))
    parts = split3(jnp.concatenate(diag))
    extra = jnp.zeros((scen_local, 16, PANELS * PW), jnp.bfloat16).at[0, :3].set(parts)
    window = jnp.concatenate([jnp.concatenate(window, axis=2), extra], axis=1)
    window = lax.psum(window, "border")
    window_diag = jnp.sum(window[0, order : order + 3].astype(jnp.float32), axis=0)
    window = window[:, :order]

    (inverse,) = factor_call(first_kernel, scen_local, order, [blocks], jnp.bfloat16, False)
    inverse, raws = lax.optimization_barrier((inverse, raws))
    packed = pack(inverse)
    inverses = [unpack(swap(packed, step)) for step in range(1, far)]
    solved_far = swap(solve(inverse, piece_of(far)), far)
    solved = [solve(inverse, piece_of(0))]
    solved += [solve(inv, raw) for inv, raw in zip(inverses, raws)]
    solved.append(solved_far)

    own = solve(inverse, window)
    core = lax.bitwise_and(border_pos, 1)
    half = scen_local // 2
    ours = cut(own, core * half, half, 0)
    panels = [own]
    for step in range(1, scen_count):
        mine = swap(ours, step)
        other = lax.ppermute(
            mine, "border", [(i, i ^ 1) for i in range(lax.axis_size("border"))]
        )
        panels += [mine, other]
    factor_inverse, factor = factor_call(
        second_kernel, PANELS, PW, [window_diag.reshape(PANELS, PW), *panels], jnp.float32, True
    )

    base = border_pos * width + scen_pos * share
    window_cols = (panel_ids[:, None] * PW + jnp.arange(PW, dtype=jnp.int32)[None, :]).reshape(1, -1)
    diag_part = cut(root_diag, scen_pos * share, share, 0)
    rows = root_rows(
        core.reshape(1), diag_part[:, None], window_cols - base, factor_inverse, solved, panels
    )
    return (rows, factor)


def solution(mesh):
    placed = (P("scen", None, "border"), P("scen", None, None), P("border"), P("scen"), P())
    return jax.shard_map(
        on_device,
        mesh=mesh,
        in_specs=placed,
        out_specs=(P("border", "scen", None), P()),
        check_vma=False,
    )
```

```python
import functools

import jax
import jax.numpy as jnp
from jax import lax
from jax.experimental import pallas as pl
from jax.experimental.pallas import tpu as pltpu
from jax.sharding import PartitionSpec as P

PW = 256
PANELS = 4
BLK = 128
SUB = 8


def eliminate(mats):
    lane1 = lax.broadcasted_iota(jnp.int32, (1, BLK), 1)
    sub8 = lax.broadcasted_iota(jnp.int32, (SUB, BLK), 0)
    lane8 = lax.broadcasted_iota(jnp.int32, (SUB, BLK), 1)
    rests = list(mats)
    done = [[] for _ in mats]
    for group in range(BLK // SUB):
        base = group * SUB
        rows = BLK - base
        cols = [
            [jnp.broadcast_to(rest[:, base + t : base + t + 1], (rows, BLK)) for t in range(SUB)]
            for rest in rests
        ]
        tops = [rest[:SUB] for rest in rests]
        lows = [rest[SUB:] for rest in rests]
        if rows > SUB:
            wide = lax.broadcasted_iota(jnp.int32, (rows - SUB, BLK), 1)
            inside = (wide >= base) & (wide < base + SUB)
            lows = [jnp.where(inside, 0.0, low) for low in lows]
        pivots = [jnp.ones((SUB, BLK), jnp.float32) for _ in mats]
        for t in range(SUB):
            for m in range(len(mats)):
                col = cols[m][t]
                pivot = col[t : t + 1, :]
                scaled = col * (1.0 / pivot)
                top = tops[m]
                row = jnp.where(lane1 == base + t, 1.0, top[t : t + 1, :])
                below = sub8 > t
                cleared = jnp.where(
                    lane8 == base + t, jnp.where(below, 0.0, 1.0), top
                )
                cleared = jnp.where((lane8 == base + t) & (sub8 < t), top, cleared)
                tops[m] = cleared - jnp.where(below, scaled[:SUB], 0.0) * row
                pivots[m] = jnp.where(sub8 == t, pivot, pivots[m])
                if rows > SUB:
                    later = (lane1 > base + t) & (lane1 < base + SUB)
                    lows[m] = lows[m] - scaled[SUB:] * jnp.where(later, 0.0, row)
                for s in range(t + 1, SUB):
                    cols[m][s] = cols[m][s] - scaled * col[s : s + 1, :]
        for m in range(len(mats)):
            done[m].append(tops[m] * lax.rsqrt(pivots[m]))
        rests = lows
    return [jnp.concatenate(part, axis=0) for part in done]


def mxu(left, right, dims):
    return lax.dot_general(
        left, right, (dims, ((), ())),
        precision=lax.Precision.HIGHEST, preferred_element_type=jnp.float32,
    )


def first_kernel(count, order, in_ref, inv_ref, work):
    work[...] = in_ref[...]
    factor_in_place(count, order, work, inv_ref, None)


def second_kernel(used, count, order, diag_ref, *refs):
    panel_refs = refs[:used]
    inv_ref, low_ref, work = refs[-3:]
    row = lax.broadcasted_iota(jnp.int32, (order, order), 0)
    col = lax.broadcasted_iota(jnp.int32, (order, order), 1)
    for p in range(count):
        total = jnp.where(row == col, diag_ref[p : p + 1, :], 0.0)
        for ref in panel_refs:
            for i in range(ref.shape[0]):
                cols = ref[i, :, p * order : (p + 1) * order]
                total = total + lax.dot_general(
                    cols, cols, (((0,), (0,)), ((), ())), preferred_element_type=jnp.float32
                )
        work[p] = total
    factor_in_place(count, order, work, inv_ref, low_ref)


def factor_in_place(count, order, work, inv_ref, low_ref):
    steps = order // BLK
    eye = (
        lax.broadcasted_iota(jnp.int32, (BLK, BLK), 0)
        == lax.broadcasted_iota(jnp.int32, (BLK, BLK), 1)
    ).astype(jnp.float32)
    tril = lax.broadcasted_iota(jnp.int32, (BLK, BLK), 0) >= lax.broadcasted_iota(
        jnp.int32, (BLK, BLK), 1
    )

    @pl.loop(0, steps)
    def _(step):
        here = pl.ds(pl.multiple_of(step * BLK, BLK), BLK)
        blocks = eliminate([work[m, here, here] for m in range(count)])
        for m in range(count):
            inverse = jnp.where(tril, blocks[m], 0.0)
            work[m, here, here] = eye
            panel = mxu(inverse, work[m, here, :], ((1,), (0,)))
            work[m, here, :] = panel
            for i in range(1, steps):
                mine = slice(i * BLK, (i + 1) * BLK)

                @pl.when(i > step)
                def _():
                    work[m, mine, here] = jnp.zeros((BLK, BLK), jnp.float32)
                    work[m, mine, :] = work[m, mine, :] - mxu(
                        panel[:, mine], panel, ((0,), (0,))
                    )

            work[m, here, here] = blocks[m]

    row = lax.broadcasted_iota(jnp.int32, (order, order), 0)
    col = lax.broadcasted_iota(jnp.int32, (order, order), 1)
    for m in range(count):
        full = work[m]
        inv_ref[m] = jnp.where(row >= col, full, 0.0).astype(inv_ref.dtype)
        if low_ref is not None:
            low_ref[m] = jnp.where(
                row > col, full.T, jnp.where(row == col, 1.0 / full, 0.0)
            )


def factor_call(body, count, order, args, inv_type, want_lower, after=()):
    shape = (count, order, order)
    out = [jax.ShapeDtypeStruct(shape, inv_type)]
    if want_lower:
        out.append(jax.ShapeDtypeStruct(shape, jnp.float32))
    return pl.pallas_call(
        functools.partial(body, count, order),
        out_shape=tuple(out),
        in_specs=[pl.BlockSpec(memory_space=pltpu.VMEM) for _ in args]
        + [pl.BlockSpec(memory_space=pl.ANY) for _ in after],
        out_specs=tuple(pl.BlockSpec(memory_space=pltpu.VMEM) for _ in out),
        scratch_shapes=[pltpu.VMEM(shape, jnp.float32)],
        compiler_params=pltpu.CompilerParams(vmem_limit_bytes=40 * 1024 * 1024),
        cost_estimate=pl.CostEstimate(
            flops=30 * 10**9, bytes_accessed=count * order * order * 16, transcendentals=0
        ),
    )(*args, *after)


def rows_kernel(pairs, half, core_ref, diag_ref, window_ref, inv_ref, *refs):
    *refs, out_ref = refs
    solved, panels = refs[:pairs], refs[pairs:]
    cols = out_ref.shape[1]
    core = core_ref[0]
    place = lax.broadcasted_iota(jnp.int32, (cols, 1), 0) + pl.program_id(0) * cols
    total = jnp.where(place == window_ref[...], diag_ref[...], 0.0)

    def gram(left, right):
        return lax.dot_general(
            left, right, (((0,), (0,)), ((), ())), preferred_element_type=jnp.float32
        )

    for k in range(pairs):
        mine, other = panels[2 * k], panels[2 * k + 1]
        for i in range(half):
            total = total + gram(solved[k][core * half + i], mine[i])
            total = total + gram(solved[k][(1 - core) * half + i], other[i])

    def parts(value):
        high = value.astype(jnp.bfloat16)
        return high, (value - high.astype(jnp.float32)).astype(jnp.bfloat16)

    def times(left, right):
        return lax.dot_general(
            left, right, (((1,), (1,)), ((), ())), preferred_element_type=jnp.float32
        )

    order = inv_ref.shape[1]
    for p in range(inv_ref.shape[0]):
        here = slice(p * order, (p + 1) * order)
        left_high, left_low = parts(total[:, here])
        high, low = parts(inv_ref[p])
        out_ref[0, :, here] = (
            times(left_low, high) + times(left_high, low) + times(left_high, high)
        )


def root_rows(core, diag, window, inverse, solved, panels):
    local, order, share = solved[0].shape
    cols = min(share, 256)
    whole = pl.BlockSpec(memory_space=pltpu.VMEM)
    return pl.pallas_call(
        functools.partial(rows_kernel, len(solved), local // 2),
        grid=(share // cols,),
        out_shape=jax.ShapeDtypeStruct((1, share, window.shape[1]), jnp.float32),
        in_specs=[
            pl.BlockSpec(memory_space=pltpu.SMEM),
            pl.BlockSpec((cols, 1), lambda i: (i, 0)),
            whole,
            whole,
        ]
        + [pl.BlockSpec((local, order, cols), lambda i: (0, 0, i)) for _ in solved]
        + [whole for _ in panels],
        out_specs=pl.BlockSpec((1, cols, window.shape[1]), lambda i: (0, i, 0)),
        compiler_params=pltpu.CompilerParams(vmem_limit_bytes=48 * 1024 * 1024),
        cost_estimate=pl.CostEstimate(
            flops=12 * 10**9, bytes_accessed=20 * 1024 * 1024, transcendentals=0
        ),
    )(core, diag, window, inverse, *solved, *panels)


def window_kernel(half, core_ref, inv_ref, window_ref, *refs):
    out_ref = refs[-1]
    order = out_ref.shape[1]
    for i in range(half):
        out_ref[i] = jnp.dot(
            inv_ref[core_ref[0] * half + i],
            window_ref[i, :order, :],
            preferred_element_type=jnp.float32,
        ).astype(out_ref.dtype)


def window_solve(core, inverse, window, after):
    half, _, cols = window.shape
    whole = pl.BlockSpec(memory_space=pltpu.VMEM)
    return pl.pallas_call(
        functools.partial(window_kernel, half),
        out_shape=jax.ShapeDtypeStruct((half, inverse.shape[1], cols), jnp.bfloat16),
        in_specs=[pl.BlockSpec(memory_space=pltpu.SMEM), whole, whole]
        + [pl.BlockSpec(memory_space=pl.ANY) for _ in after],
        out_specs=whole,
        compiler_params=pltpu.CompilerParams(vmem_limit_bytes=24 * 1024 * 1024),
        cost_estimate=pl.CostEstimate(
            flops=2 * half * inverse.shape[1] ** 2 * cols,
            bytes_accessed=3 * 1024 * 1024, transcendentals=0,
        ),
    )(core, inverse, window, *after)


def cut(array, start, size, axis):
    return lax.dynamic_slice_in_dim(array, start, size, axis, allow_negative_indices=False)


def split3(value):
    high = value.astype(jnp.bfloat16)
    rest = value - high.astype(jnp.float32)
    middle = rest.astype(jnp.bfloat16)
    low = (rest - middle.astype(jnp.float32)).astype(jnp.bfloat16)
    return jnp.stack([high, middle, low])


def pack(inverse):
    half = inverse.shape[1] // 2
    return jnp.concatenate([inverse[:, :half, :half], inverse[:, half:, :]], axis=2)


def unpack(packed):
    half = packed.shape[1]
    top = jnp.concatenate([packed[:, :, :half], jnp.zeros_like(packed[:, :, :half])], axis=2)
    return jnp.concatenate([top, packed[:, :, half:]], axis=1)


def on_device(border, blocks, root_diag, live_rows, panel_ids):
    scen_local, order, width = border.shape
    scen_count = lax.axis_size("scen")
    far = scen_count - 1
    share = width // scen_count
    border_pos = lax.axis_index("border")
    scen_pos = lax.axis_index("scen")
    slabs = width // PW
    levels = jnp.arange(order, dtype=jnp.int32)
    keep = levels[None, :, None] >= (order - live_rows)[:, None, None]

    def swap(value, step):
        return lax.ppermute(value, "scen", [(i, i ^ step) for i in range(scen_count)])

    def piece_of(step):
        cols = cut(border, (scen_pos ^ step) * share, share, 2)
        return jnp.where(keep, cols, jnp.zeros_like(cols))

    def solve(inv, columns):
        return jnp.einsum(
            "ikr,irc->ikc", inv, columns, preferred_element_type=jnp.float32
        ).astype(jnp.bfloat16)

    raws = [swap(piece_of(step), step) for step in range(1, far)]

    window = []
    diag = []
    for position in range(PANELS):
        chosen = panel_ids[position]
        mine = lax.div(chosen, slabs) == border_pos
        offset = lax.rem(chosen, slabs) * PW
        cols = cut(border, offset, PW, 2)
        window.append(jnp.where(keep & mine, cols, jnp.zeros_like(cols)))
        part = cut(root_diag, offset, PW, 0)
        diag.append(jnp.where(mine, part, jnp.zeros_like(part)))
    parts = split3(jnp.concatenate(diag))
    extra = jnp.concatenate([parts, jnp.zeros((13, PANELS * PW), jnp.bfloat16)])
    extra = jnp.broadcast_to(extra[None], (scen_local, 16, PANELS * PW))
    window = jnp.concatenate([jnp.concatenate(window, axis=2), extra], axis=1)
    core = lax.bitwise_and(border_pos, 1)
    half = scen_local // 2
    border_count = lax.axis_size("border")

    def cross(value):
        return lax.ppermute(value, "border", [(i, i ^ 1) for i in range(border_count)])

    window = cut(window, core * half, half, 0) + cross(cut(window, (1 - core) * half, half, 0))
    groups = [list(range(c, border_count, 2)) for c in range(2)]
    window = lax.psum(window, "border", axis_index_groups=groups)
    window_diag = jnp.sum(window[0, order : order + 3].astype(jnp.float32), axis=0)

    (inverse,) = factor_call(first_kernel, scen_local, order, [blocks], jnp.bfloat16, False)
    inverse, raws = lax.optimization_barrier((inverse, raws))
    packed = pack(inverse)
    received = [swap(packed, step) for step in range(1, far)]
    far_solved = solve(inverse, piece_of(far))
    own_solved = solve(inverse, piece_of(0))

    ours = window_solve(core.reshape(1), inverse, window, [*received, far_solved])
    panels = [ours, cross(ours)]
    for step in range(1, scen_count):
        mine = swap(ours, step)
        panels += [mine, cross(mine)]
    near = [solve(unpack(part), raw) for part, raw in zip(received, raws)]
    factor_inverse, factor = factor_call(
        functools.partial(second_kernel, len(panels)),
        PANELS, PW, [window_diag.reshape(PANELS, PW), *panels], jnp.float32, True,
        after=[own_solved, *near],
    )
    solved = [own_solved, *near, swap(far_solved, far)]

    base = border_pos * width + scen_pos * share
    window_cols = (panel_ids[:, None] * PW + jnp.arange(PW, dtype=jnp.int32)[None, :]).reshape(1, -1)
    diag_part = cut(root_diag, scen_pos * share, share, 0)
    rows = root_rows(
        core.reshape(1), diag_part[:, None], window_cols - base, factor_inverse, solved, panels
    )
    return (rows, factor)


def solution(mesh):
    placed = (P("scen", None, "border"), P("scen", None, None), P("border"), P("scen"), P())
    return jax.shard_map(
        on_device,
        mesh=mesh,
        in_specs=placed,
        out_specs=(P("border", "scen", None), P()),
        check_vma=False,
    )
```

```python
import functools

import jax
import jax.numpy as jnp
from jax import lax
from jax.experimental import pallas as pl
from jax.experimental.pallas import tpu as pltpu
from jax.sharding import PartitionSpec as P

PW = 256
PANELS = 4
BLK = 128
SUB = 8


def eliminate(mats):
    lane1 = lax.broadcasted_iota(jnp.int32, (1, BLK), 1)
    sub8 = lax.broadcasted_iota(jnp.int32, (SUB, BLK), 0)
    lane8 = lax.broadcasted_iota(jnp.int32, (SUB, BLK), 1)
    rests = list(mats)
    done = [[] for _ in mats]
    for group in range(BLK // SUB):
        base = group * SUB
        rows = BLK - base
        cols = [
            [jnp.broadcast_to(rest[:, base + t : base + t + 1], (rows, BLK)) for t in range(SUB)]
            for rest in rests
        ]
        tops = [rest[:SUB] for rest in rests]
        lows = [rest[SUB:] for rest in rests]
        if rows > SUB:
            wide = lax.broadcasted_iota(jnp.int32, (rows - SUB, BLK), 1)
            inside = (wide >= base) & (wide < base + SUB)
            lows = [jnp.where(inside, 0.0, low) for low in lows]
        pivots = [jnp.ones((SUB, BLK), jnp.float32) for _ in mats]
        for t in range(SUB):
            for m in range(len(mats)):
                col = cols[m][t]
                pivot = col[t : t + 1, :]
                scaled = col * (1.0 / pivot)
                top = tops[m]
                row = jnp.where(lane1 == base + t, 1.0, top[t : t + 1, :])
                below = sub8 > t
                cleared = jnp.where(
                    lane8 == base + t, jnp.where(below, 0.0, 1.0), top
                )
                cleared = jnp.where((lane8 == base + t) & (sub8 < t), top, cleared)
                tops[m] = cleared - jnp.where(below, scaled[:SUB], 0.0) * row
                pivots[m] = jnp.where(sub8 == t, pivot, pivots[m])
                if rows > SUB:
                    later = (lane1 > base + t) & (lane1 < base + SUB)
                    lows[m] = lows[m] - scaled[SUB:] * jnp.where(later, 0.0, row)
                for s in range(t + 1, SUB):
                    cols[m][s] = cols[m][s] - scaled * col[s : s + 1, :]
        for m in range(len(mats)):
            done[m].append(tops[m] * lax.rsqrt(pivots[m]))
        rests = lows
    return [jnp.concatenate(part, axis=0) for part in done]


def mxu(left, right, dims):
    return lax.dot_general(
        left, right, (dims, ((), ())),
        precision=lax.Precision.HIGHEST, preferred_element_type=jnp.float32,
    )


def first_kernel(count, order, in_ref, inv_ref, work):
    work[...] = in_ref[...]
    factor_in_place(count, order, work, inv_ref, None)


def second_kernel(used, count, order, diag_ref, *refs):
    panel_refs = refs[:used]
    inv_ref, low_ref, work = refs[-3:]
    row = lax.broadcasted_iota(jnp.int32, (order, order), 0)
    col = lax.broadcasted_iota(jnp.int32, (order, order), 1)
    for p in range(count):
        total = jnp.where(row == col, diag_ref[p : p + 1, :], 0.0)
        for ref in panel_refs:
            for i in range(ref.shape[0]):
                cols = ref[i, :, p * order : (p + 1) * order]
                total = total + lax.dot_general(
                    cols, cols, (((0,), (0,)), ((), ())), preferred_element_type=jnp.float32
                )
        work[p] = total
    factor_in_place(count, order, work, inv_ref, low_ref)


def factor_in_place(count, order, work, inv_ref, low_ref):
    steps = order // BLK
    eye = (
        lax.broadcasted_iota(jnp.int32, (BLK, BLK), 0)
        == lax.broadcasted_iota(jnp.int32, (BLK, BLK), 1)
    ).astype(jnp.float32)
    tril = lax.broadcasted_iota(jnp.int32, (BLK, BLK), 0) >= lax.broadcasted_iota(
        jnp.int32, (BLK, BLK), 1
    )

    @pl.loop(0, steps)
    def _(step):
        here = pl.ds(pl.multiple_of(step * BLK, BLK), BLK)
        blocks = eliminate([work[m, here, here] for m in range(count)])
        for m in range(count):
            inverse = jnp.where(tril, blocks[m], 0.0)
            work[m, here, here] = eye
            panel = mxu(inverse, work[m, here, :], ((1,), (0,)))
            work[m, here, :] = panel
            for i in range(1, steps):
                mine = slice(i * BLK, (i + 1) * BLK)

                @pl.when(i > step)
                def _():
                    work[m, mine, here] = jnp.zeros((BLK, BLK), jnp.float32)
                    work[m, mine, :] = work[m, mine, :] - mxu(
                        panel[:, mine], panel, ((0,), (0,))
                    )

            work[m, here, here] = blocks[m]

    row = lax.broadcasted_iota(jnp.int32, (order, order), 0)
    col = lax.broadcasted_iota(jnp.int32, (order, order), 1)
    for m in range(count):
        full = work[m]
        inv_ref[m] = jnp.where(row >= col, full, 0.0).astype(inv_ref.dtype)
        if low_ref is not None:
            low_ref[m] = jnp.where(
                row > col, full.T, jnp.where(row == col, 1.0 / full, 0.0)
            )


def factor_call(body, count, order, args, inv_type, want_lower, after=()):
    shape = (count, order, order)
    out = [jax.ShapeDtypeStruct(shape, inv_type)]
    if want_lower:
        out.append(jax.ShapeDtypeStruct(shape, jnp.float32))
    return pl.pallas_call(
        functools.partial(body, count, order),
        out_shape=tuple(out),
        in_specs=[pl.BlockSpec(memory_space=pltpu.VMEM) for _ in args]
        + [pl.BlockSpec(memory_space=pl.ANY) for _ in after],
        out_specs=tuple(pl.BlockSpec(memory_space=pltpu.VMEM) for _ in out),
        scratch_shapes=[pltpu.VMEM(shape, jnp.float32)],
        compiler_params=pltpu.CompilerParams(vmem_limit_bytes=40 * 1024 * 1024),
        cost_estimate=pl.CostEstimate(
            flops=30 * 10**9, bytes_accessed=count * order * order * 16, transcendentals=0
        ),
    )(*args, *after)


def rows_kernel(pairs, half, core_ref, diag_ref, window_ref, inv_ref, *refs):
    *refs, out_ref = refs
    solved, panels = refs[:pairs], refs[pairs:]
    cols = out_ref.shape[1]
    core = core_ref[0]
    place = lax.broadcasted_iota(jnp.int32, (cols, 1), 0) + pl.program_id(0) * cols
    total = jnp.where(place == window_ref[...], diag_ref[...], 0.0)

    def gram(left, right):
        return lax.dot_general(
            left, right, (((0,), (0,)), ((), ())), preferred_element_type=jnp.float32
        )

    for k in range(pairs):
        mine, other = panels[2 * k], panels[2 * k + 1]
        for i in range(half):
            total = total + gram(solved[k][core * half + i], mine[i])
            total = total + gram(solved[k][(1 - core) * half + i], other[i])

    def parts(value):
        high = value.astype(jnp.bfloat16)
        return high, (value - high.astype(jnp.float32)).astype(jnp.bfloat16)

    def times(left, right):
        return lax.dot_general(
            left, right, (((1,), (1,)), ((), ())), preferred_element_type=jnp.float32
        )

    order = inv_ref.shape[1]
    for p in range(inv_ref.shape[0]):
        here = slice(p * order, (p + 1) * order)
        left_high, left_low = parts(total[:, here])
        high, low = parts(inv_ref[p])
        out_ref[0, :, here] = (
            times(left_low, high) + times(left_high, low) + times(left_high, high)
        )


def root_rows(core, diag, window, inverse, solved, panels):
    local, order, share = solved[0].shape
    cols = min(share, 256)
    whole = pl.BlockSpec(memory_space=pltpu.VMEM)
    return pl.pallas_call(
        functools.partial(rows_kernel, len(solved), local // 2),
        grid=(share // cols,),
        out_shape=jax.ShapeDtypeStruct((1, share, window.shape[1]), jnp.float32),
        in_specs=[
            pl.BlockSpec(memory_space=pltpu.SMEM),
            pl.BlockSpec((cols, 1), lambda i: (i, 0)),
            whole,
            whole,
        ]
        + [pl.BlockSpec((local, order, cols), lambda i: (0, 0, i)) for _ in solved]
        + [whole for _ in panels],
        out_specs=pl.BlockSpec((1, cols, window.shape[1]), lambda i: (0, i, 0)),
        compiler_params=pltpu.CompilerParams(vmem_limit_bytes=48 * 1024 * 1024),
        cost_estimate=pl.CostEstimate(
            flops=12 * 10**9, bytes_accessed=20 * 1024 * 1024, transcendentals=0
        ),
    )(core, diag, window, inverse, *solved, *panels)


def window_kernel(half, core_ref, inv_ref, window_ref, *refs):
    out_ref = refs[-1]
    order = out_ref.shape[1]
    for i in range(half):
        out_ref[i] = jnp.dot(
            inv_ref[core_ref[0] * half + i],
            window_ref[i, :order, :],
            preferred_element_type=jnp.float32,
        ).astype(out_ref.dtype)


def window_solve(core, inverse, window, after):
    half, _, cols = window.shape
    whole = pl.BlockSpec(memory_space=pltpu.VMEM)
    return pl.pallas_call(
        functools.partial(window_kernel, half),
        out_shape=jax.ShapeDtypeStruct((half, inverse.shape[1], cols), jnp.bfloat16),
        in_specs=[pl.BlockSpec(memory_space=pltpu.SMEM), whole, whole]
        + [pl.BlockSpec(memory_space=pl.ANY) for _ in after],
        out_specs=whole,
        compiler_params=pltpu.CompilerParams(vmem_limit_bytes=24 * 1024 * 1024),
        cost_estimate=pl.CostEstimate(
            flops=2 * half * inverse.shape[1] ** 2 * cols,
            bytes_accessed=3 * 1024 * 1024, transcendentals=0,
        ),
    )(core, inverse, window, *after)


def cut(array, start, size, axis):
    return lax.dynamic_slice_in_dim(array, start, size, axis, allow_negative_indices=False)


def split3(value):
    high = value.astype(jnp.bfloat16)
    rest = value - high.astype(jnp.float32)
    middle = rest.astype(jnp.bfloat16)
    low = (rest - middle.astype(jnp.float32)).astype(jnp.bfloat16)
    return jnp.stack([high, middle, low])


def pack(inverse):
    half = inverse.shape[1] // 2
    return jnp.concatenate([inverse[:, :half, :half], inverse[:, half:, :]], axis=2)


def unpack(packed):
    half = packed.shape[1]
    top = jnp.concatenate([packed[:, :, :half], jnp.zeros_like(packed[:, :, :half])], axis=2)
    return jnp.concatenate([top, packed[:, :, half:]], axis=1)


def on_device(border, blocks, root_diag, live_rows, panel_ids):
    scen_local, order, width = border.shape
    scen_count = lax.axis_size("scen")
    far = scen_count - 1
    share = width // scen_count
    border_pos = lax.axis_index("border")
    scen_pos = lax.axis_index("scen")
    slabs = width // PW
    levels = jnp.arange(order, dtype=jnp.int32)
    keep = levels[None, :, None] >= (order - live_rows)[:, None, None]

    def swap(value, step):
        return lax.ppermute(value, "scen", [(i, i ^ step) for i in range(scen_count)])

    def piece_of(step):
        cols = cut(border, (scen_pos ^ step) * share, share, 2)
        return jnp.where(keep, cols, jnp.zeros_like(cols))

    def solve(inv, columns):
        return jnp.einsum(
            "ikr,irc->ikc", inv, columns, preferred_element_type=jnp.float32
        ).astype(jnp.bfloat16)

    raws = [swap(piece_of(step), step) for step in range(1, far)]

    window = []
    diag = []
    for position in range(PANELS):
        chosen = panel_ids[position]
        mine = lax.div(chosen, slabs) == border_pos
        offset = lax.rem(chosen, slabs) * PW
        cols = cut(border, offset, PW, 2)
        window.append(jnp.where(keep & mine, cols, jnp.zeros_like(cols)))
        part = cut(root_diag, offset, PW, 0)
        diag.append(jnp.where(mine, part, jnp.zeros_like(part)))
    parts = split3(jnp.concatenate(diag))
    extra = jnp.concatenate([parts, jnp.zeros((13, PANELS * PW), jnp.bfloat16)])
    extra = jnp.broadcast_to(extra[None], (scen_local, 16, PANELS * PW))
    window = jnp.concatenate([jnp.concatenate(window, axis=2), extra], axis=1)
    core = lax.bitwise_and(border_pos, 1)
    half = scen_local // 2
    border_count = lax.axis_size("border")

    def cross(value):
        return lax.ppermute(value, "border", [(i, i ^ 1) for i in range(border_count)])

    window = cut(window, core * half, half, 0) + cross(cut(window, (1 - core) * half, half, 0))
    groups = [list(range(c, border_count, 2)) for c in range(2)]
    window = lax.psum(window, "border", axis_index_groups=groups)
    window_diag = jnp.sum(window[0, order : order + 3].astype(jnp.float32), axis=0)

    (inverse,) = factor_call(first_kernel, scen_local, order, [blocks], jnp.bfloat16, False)
    inverse, raws = lax.optimization_barrier((inverse, raws))
    packed = pack(inverse)
    received = [swap(packed, step) for step in range(1, far)]
    far_solved = solve(inverse, piece_of(far))
    own_solved = solve(inverse, piece_of(0))

    ours = window_solve(core.reshape(1), inverse, window, [*received, far_solved])
    panels = [ours, cross(ours)]
    arrived = [swap(ours, step) for step in range(1, scen_count)]
    arrived, far_solved = lax.optimization_barrier((arrived, far_solved))
    for mine in arrived:
        panels += [mine, cross(mine)]
    near = [solve(unpack(part), raw) for part, raw in zip(received, raws)]
    factor_inverse, factor = factor_call(
        functools.partial(second_kernel, len(panels)),
        PANELS, PW, [window_diag.reshape(PANELS, PW), *panels], jnp.float32, True,
        after=[own_solved, *near],
    )
    solved = [own_solved, *near, swap(far_solved, far)]

    base = border_pos * width + scen_pos * share
    window_cols = (panel_ids[:, None] * PW + jnp.arange(PW, dtype=jnp.int32)[None, :]).reshape(1, -1)
    diag_part = cut(root_diag, scen_pos * share, share, 0)
    rows = root_rows(
        core.reshape(1), diag_part[:, None], window_cols - base, factor_inverse, solved, panels
    )
    return (rows, factor)


def solution(mesh):
    placed = (P("scen", None, "border"), P("scen", None, None), P("border"), P("scen"), P())
    return jax.shard_map(
        on_device,
        mesh=mesh,
        in_specs=placed,
        out_specs=(P("border", "scen", None), P()),
        check_vma=False,
    )
```
